32 devices in a mesh: energy: 2 (over x), row: 4 (over z), col: 4 (over y, core).
Axes of the slice: x: 2, y: 2, z: 4, core: 2. Of those that a mesh axis runs over, the one named last changes fastest.
Arguments:
- object_field: float32 [2, 32, 1024, 1024], P(None, 'energy', 'row', 'col'), may hold values from -6 to 6
- probe_field: float32 [2, 32, 256, 256], P(None, 'energy'), may hold values from -5 to 5
- amplitudes: float32 [32, 4, 4, 4, 256, 256], P('energy', 'row', 'col'), may hold values from 0 to 3
- kk_kernel: float32 [2, 2, 32, 32], replicated, may hold values from -0.75 to 0.75
- offsets: int32 [4, 4, 4, 2], P('row', 'col'), may hold values from 0 to 128, as said below
Outputs:
- blended: float32 [2, 32, 1024, 1024], P(None, 'energy', 'row', 'col')
- new_probe: float32 [2, 32, 256, 256], P(None, 'energy')
The draws below stay inside these ranges and needn't reach their ends.
Inputs may be any that keep to these rules, and one draw needn't show every extreme that they name: `offsets`: position k of every tile starts within 32 of 0 for k = 0, 1 and within 32 below 128 for k = 2, 3 in rows; in columns likewise, near 0 for even k and near the top for odd k.
All inputs are finite; a program needn't handle non-finite values.
Results may differ from the reference program's by a relative error of at most 0.0001.
Values sent between devices are 32-bit elements; how exact they have to be, the bound alone decides.
No kernel may reach another device: no remote copies, remote signals or barrier semaphores. Data moves between devices by JAX's collectives and lax.ppermute only.
A program may use at most 320 MiB of HBM per device.

```python
import math
import jax
import jax.numpy as jnp
from jax import lax

E = 32
WIN = 256
TILE = 256
HALO = 64
JITTER = 32
TR = 4
TC = 4
NY = 1024
NX = 1024


def draw_offsets(key, part):
    jitter = jax.random.randint(key, (TR, TC, 4, 2), 0, JITTER + 1, dtype=jnp.int32)
    jitter = jitter.at[0, 0, 0, :].set(0).at[0, 0, 3, :].set(0)
    position = jnp.arange(4, dtype=jnp.int32)
    far_side = jnp.stack([position >= 2, position % 2 == 1], axis=1)
    reach = TILE + 2 * HALO - WIN
    return jnp.where(far_side[None, None], reach - jitter, jitter).astype(jnp.int32)


def block_scale(key, dims, cuts, least, top_value):
    def one(dim, shards_of):
        steps = jax.random.uniform(jax.random.fold_in(jax.random.fold_in(key, 6), dim), (shards_of,), jnp.float32, least / len(cuts), top_value / len(cuts))
        return jnp.repeat(jnp.exp(steps), dims[dim] // shards_of).reshape((-1,) + (1,) * (len(dims) - dim - 1))

    level = one(*cuts[0])
    for cut in cuts[1:]:
        level = level * one(*cut)
    return level


def centred(stream_key, shape, width, limit, shards=(), kind=jnp.bfloat16):
    factor_of = block_scale(stream_key, shape, shards, -0.22, 0.18) if shards else 1.0
    entries = jax.random.normal(stream_key, shape, jnp.float32) * width * factor_of
    return jnp.minimum(jnp.maximum(entries, -limit), limit).astype(kind)


def setup_inputs(seed: int = 0) -> dict:
    key_list = jax.random.split(jax.random.key(seed), 6)
    object_field = centred(key_list[0], (2, E, NY, NX), 1.0, 6.0, ((1, 2), (2, 4), (3, 4)), jnp.float32)
    probe_field = centred(key_list[1], (2, E, WIN, WIN), 0.7, 5.0, ((1, 2),), jnp.float32)
    amplitudes = jnp.clip(3.0 * jax.random.uniform(key_list[2], (E, TR, TC, 4, WIN, WIN), jnp.float32) ** block_scale(key_list[2], (E, TR, TC, 4, WIN, WIN), ((0, 2), (1, 4), (2, 4)), -0.2, 0.2), 0.0, 3.0)
    kk_kernel = centred(key_list[3], (2, 2, E, E), (2 * E) ** -0.5, 0.75, (), jnp.float32)
    offsets = draw_offsets(jax.random.fold_in(key_list[5], 71), 0)
    return {"object_field": object_field, "probe_field": probe_field, "amplitudes": amplitudes, "kk_kernel": kk_kernel, "offsets": offsets}


PRECISE = lax.Precision.HIGHEST
STEP = 0.25
PROBE_STEP = 0.5
FLOOR = 0.25

def dft_tables(length):
    counter = jnp.arange(length, dtype=jnp.int32)
    phases = counter[:, None] * counter[None, :] % length
    angles = phases.astype(jnp.float32) * (2.0 * math.pi / length)
    factor = 1.0 / math.sqrt(length)
    return (jnp.cos(angles) * factor, -jnp.sin(angles) * factor)

def left_product(cos_table, sin_table, real_part, imag_part):

    def multiply(matrix, field):
        return jnp.einsum('uv,evw->euw', matrix, field, precision=PRECISE)
    return (multiply(cos_table, real_part) - multiply(sin_table, imag_part), multiply(cos_table, imag_part) + multiply(sin_table, real_part))

def right_product(cos_table, sin_table, real_part, imag_part):

    def multiply(field, matrix):
        return jnp.einsum('euv,vw->euw', field, matrix, precision=PRECISE)
    return (multiply(real_part, cos_table) - multiply(imag_part, sin_table), multiply(real_part, sin_table) + multiply(imag_part, cos_table))

def transform(cos_table, sin_table, real_part, imag_part):
    real_part, imag_part = left_product(cos_table, sin_table, real_part, imag_part)
    return right_product(cos_table, sin_table, real_part, imag_part)

def position_update(window, probe_field, measured, cos_table, sin_table):
    probe_real, probe_imag = (probe_field[0], probe_field[1])
    window_real, window_imag = (window[0], window[1])
    exit_real = probe_real * window_real - probe_imag * window_imag
    exit_imag = probe_real * window_imag + probe_imag * window_real
    far_real, far_imag = transform(cos_table, sin_table, exit_real, exit_imag)
    modulus = jnp.sqrt(far_real * far_real + far_imag * far_imag)
    rescale = measured / jnp.maximum(modulus, FLOOR)
    back_real, back_imag = transform(cos_table, -sin_table, far_real * rescale, far_imag * rescale)
    diff_real = exit_real - back_real
    diff_imag = exit_imag - back_imag
    object_step = jnp.stack([probe_real * diff_real + probe_imag * diff_imag, probe_real * diff_imag - probe_imag * diff_real])
    probe_step = jnp.stack([window_real * diff_real + window_imag * diff_imag, window_real * diff_imag - window_imag * diff_real])
    return (object_step, probe_step)

def reference(object_field, probe_field, amplitudes, kk_kernel, offsets):
    cos_table, sin_table = dft_tables(WIN)
    padded = jnp.pad(object_field, ((0, 0), (0, 0), (HALO, HALO), (HALO, HALO)))
    anchor = jnp.zeros((), jnp.int32)
    shape = (2, E, WIN, WIN)

    def tile_step(tile_number, running):
        gradient, probe_grad = running
        tile_number = jnp.asarray(tile_number).astype(jnp.int32)
        row_tile = tile_number // TC
        col_tile = tile_number % TC
        for position in range(4):
            row_start = (row_tile * TILE + offsets[row_tile, col_tile, position, 0]).astype(jnp.int32)
            col_start = (col_tile * TILE + offsets[row_tile, col_tile, position, 1]).astype(jnp.int32)
            corner = (anchor, anchor, row_start, col_start)
            window = lax.dynamic_slice(padded, corner, shape)
            measured = amplitudes[:, row_tile, col_tile, position]
            object_step, probe_step = position_update(window, probe_field, measured, cos_table, sin_table)
            current = lax.dynamic_slice(gradient, corner, shape)
            gradient = lax.dynamic_update_slice(gradient, current + object_step, corner)
            probe_grad = probe_grad + probe_step
        return (gradient, probe_grad)
    start_state = (jnp.zeros_like(padded), jnp.zeros_like(probe_field))
    gradient, probe_grad = lax.fori_loop(0, TR * TC, tile_step, start_state)
    interior = gradient[:, :, HALO:HALO + NY, HALO:HALO + NX]
    stepped = object_field - STEP * interior
    new_probe = probe_field - PROBE_STEP / (4 * TR * TC) * probe_grad
    blended = stepped + jnp.einsum('abef,bfyx->aeyx', kk_kernel, stepped, precision=PRECISE)
    return (blended, new_probe)
```

```python
import math

import jax
import jax.numpy as jnp
import ml_dtypes
import numpy as np
from jax import lax
from jax.experimental import pallas as pl
from jax.experimental.pallas import tpu as pltpu
from jax.sharding import PartitionSpec as P

HALO = 64
LANES = 128
SUB = 8
STEP = 0.25
PROBE_STEP = 0.5
FLOOR = 0.25
PARTS = (2, 4, 5, 5)
VMEM = 56 * 2**20


def chunks_of(energies):
    if energies == sum(PARTS):
        sizes = PARTS
    else:
        sizes = (1,) * energies
    return [(sum(sizes[:i]), size) for i, size in enumerate(sizes)]


def split(x):
    hi = x.astype(jnp.bfloat16)
    return hi, (x - hi.astype(jnp.float32)).astype(jnp.bfloat16)


def dft_parts(length):
    half = length // 2
    pixel = np.arange(half)
    even = pixel - pixel % 2 + half * (pixel % 2)
    out = []
    for freqs in (even, even + 1):
        angle = (freqs[:, None] * pixel[None, :] % length) * (2.0 * math.pi / length)
        c, s = np.cos(angle) / math.sqrt(length), np.sin(angle) / math.sqrt(length)
        m = np.block([[c, s], [-s, c]])
        hi = m.astype(np.float32).astype(ml_dtypes.bfloat16)
        lo = (m - hi.astype(np.float64)).astype(np.float32).astype(ml_dtypes.bfloat16)
        out.append((hi, lo))
    even, odd = out
    wide = lambda m: np.concatenate([m[0], m[0], m[1]], axis=1)
    tall = lambda m: np.concatenate([m[0], m[0], m[1]], axis=0)
    t = lambda m: (m[0].T, m[1].T)
    left = np.stack([wide(even), wide(odd), wide(t(even)), wide(t(odd))])
    right = np.stack([tall(t(even)), tall(t(odd)), tall(even), tall(odd)])
    return left, right


def dot(a, b):
    return jnp.dot(a, b, preferred_element_type=jnp.float32)


def gradient_kernel(
    offs, obj, top, bot, lft, rgt, probe, amp, left, right, gout, gl, gr, pg, ext, grad
):
    win = probe.shape[2]
    tile = obj.shape[2]
    half = win // 2
    rows = tile + 2 * HALO
    mid = rows // 2
    lane = lax.broadcasted_iota(jnp.int32, (win, LANES), 1)
    for p in range(2):
        for j in range(tile // LANES):
            cols = slice(j * LANES, (j + 1) * LANES)
            ext[p, 1 + j, 0:HALO] = top[p, 0, :, cols]
            ext[p, 1 + j, HALO : HALO + tile] = obj[p, 0, :, cols]
            ext[p, 1 + j, HALO + tile : rows] = bot[p, 0, :, cols]
        packed = lft[p, 0]
        ext[p, 0, 0:mid] = pltpu.roll(packed, HALO, 1)
        ext[p, 0, mid:rows] = packed
        packed = rgt[p, 0]
        ext[p, 3, 0:mid] = packed
        ext[p, 3, mid:rows] = pltpu.roll(packed, HALO, 1)
    grad[...] = jnp.zeros_like(grad)
    pg[...] = jnp.zeros_like(pg)

    def window_of(k):
        a = offs[2 * k]
        b = offs[2 * k + 1] + HALO
        base = b // LANES
        r = b % LANES
        back = (LANES - r) % LANES
        return a, base, r, back

    def position(k):
        a, base, r, back = window_of(k)
        keep = lane < LANES - r
        def load(p):
            v = [pltpu.roll(ext[p, base + j, pl.ds(a, win), :], back, 1) for j in range(3)]
            return jnp.concatenate([jnp.where(keep, v[0], v[1]), jnp.where(keep, v[1], v[2])], axis=1)
        wr, wi = load(0), load(1)
        pr, pi = probe[0, 0], probe[1, 0]
        er = pr * wr - pi * wi
        ei = pr * wi + pi * wr

        def lmul(which, top_, bottom_):
            hi, lo = split(jnp.concatenate([top_, bottom_], axis=0))
            return dot(left[which], jnp.concatenate([hi, lo, hi], axis=0))

        def rmul(which, l_, r_):
            hi, lo = split(jnp.concatenate([l_, r_], axis=1))
            return dot(jnp.concatenate([hi, lo, hi], axis=1), right[which])

        ze = lmul(0, er[:half] + er[half:], ei[:half] + ei[half:])
        zo = lmul(1, er[:half] - er[half:], ei[:half] - ei[half:])
        zr = jnp.concatenate([ze[:half], zo[:half]], axis=0)
        zi = jnp.concatenate([ze[half:], zo[half:]], axis=0)
        ye = rmul(0, zr[:, :half] + zr[:, half:], zi[:, :half] + zi[:, half:])
        yo = rmul(1, zr[:, :half] - zr[:, half:], zi[:, :half] - zi[:, half:])
        meas = amp[0, 0, 0, k]
        groups = (half // 8, 8, win)
        mt, mb = meas[:half].reshape(groups), meas[half:].reshape(groups)
        odd_row = lax.broadcasted_iota(jnp.int32, groups, 1) % 2 == 1
        meas = jnp.concatenate(
            [
                jnp.where(odd_row, pltpu.roll(mb, 1, 1), mt).reshape(half, win),
                jnp.where(odd_row, mb, pltpu.roll(mt, 7, 1)).reshape(half, win),
            ],
            axis=0,
        )
        odd = lane % 2 == 1
        ml, mr = meas[:, :half], meas[:, half:]
        me = jnp.where(odd, pltpu.roll(mr, 1, 1), ml)
        mo = jnp.where(odd, mr, pltpu.roll(ml, LANES - 1, 1))

        def fix(y, m_):
            fr, fi = y[:, :half], y[:, half:]
            s = m_ * lax.rsqrt(jnp.maximum(fr * fr + fi * fi, FLOOR * FLOOR))
            return fr * s, fi * s

        te = rmul(2, *fix(ye, me))
        to = rmul(3, *fix(yo, mo))
        sr, dr = te[:, :half] + to[:, :half], te[:, :half] - to[:, :half]
        si, di = te[:, half:] + to[:, half:], te[:, half:] - to[:, half:]
        xr = jnp.concatenate([sr, dr], axis=1)
        xi = jnp.concatenate([si, di], axis=1)
        be = lmul(2, xr[:half], xi[:half])
        bo = lmul(3, xr[half:], xi[half:])
        br = jnp.concatenate([be[:half] + bo[:half], be[:half] - bo[:half]], axis=0)
        bi = jnp.concatenate([be[half:] + bo[half:], be[half:] - bo[half:]], axis=0)
        dr, di = er - br, ei - bi
        pg[0, 0] += wr * dr + wi * di
        pg[1, 0] += wr * di - wi * dr
        steps = (pr * dr + pi * di, pr * di - pi * dr)
        below = lane < r
        for p in range(2):
            u = pltpu.roll(steps[p][:, :LANES], r, 1)
            v = pltpu.roll(steps[p][:, LANES:], r, 1)
            grad[p, base, pl.ds(a, win), :] += jnp.where(below, 0.0, u)
            grad[p, base + 1, pl.ds(a, win), :] += jnp.where(below, u, v)
            grad[p, base + 2, pl.ds(a, win), :] += jnp.where(below, v, 0.0)

    for k in range(amp.shape[3]):
        position(k)
    first = lax.broadcasted_iota(jnp.int32, (mid, LANES), 1) < HALO
    for p in range(2):
        for j in range(tile // LANES):
            gout[p, 0, :, j * LANES : (j + 1) * LANES] = grad[p, 1 + j]
        edge = grad.at[p, 0]
        gl[p, 0] = jnp.where(first, pltpu.roll(edge[0:mid], HALO, 1), edge[mid:rows])
        edge = grad.at[p, 3]
        gr[p, 0] = jnp.where(first, edge[0:mid], pltpu.roll(edge[mid:rows], HALO, 1))


def params():
    return pltpu.CompilerParams(vmem_limit_bytes=VMEM)


def cost(flops, moved):
    return pl.CostEstimate(flops=int(flops), bytes_accessed=int(moved), transcendentals=0)


def plane(*shape):
    return pl.BlockSpec((2, 1) + shape, lambda e, *_: (0, e, 0, 0))


def later(first, *shape):
    return pl.BlockSpec((2, 1) + shape, lambda e, *_: (0, first + e, 0, 0))


def struct(*shape):
    return jax.ShapeDtypeStruct(shape, jnp.float32)


def gradient_call(offs, obj, top, bot, lft, rgt, probe, amp, left, right, first, count):
    win, tile = probe.shape[2], obj.shape[2]
    rows = tile + 2 * HALO
    side = (rows // 2, LANES)
    frame = pltpu.VMEM((2, tile // LANES + 2, rows, LANES), jnp.float32)
    whole = lambda m: pl.BlockSpec(m.shape, lambda e, *_: (0, 0, 0))
    return pl.pallas_call(
        gradient_kernel,
        grid_spec=pltpu.PrefetchScalarGridSpec(
            num_scalar_prefetch=1,
            grid=(count,),
            in_specs=[
                later(first, tile, tile),
                plane(HALO, tile),
                plane(HALO, tile),
                plane(*side),
                plane(*side),
                later(first, win, win),
                pl.BlockSpec((1, 1, 1) + amp.shape[3:], lambda e, *_: (first + e, 0, 0, 0, 0, 0)),
                whole(left),
                whole(right),
            ],
            out_specs=[plane(rows, tile), plane(*side), plane(*side), plane(win, win)],
            scratch_shapes=[frame, frame],
        ),
        out_shape=[
            struct(2, count, rows, tile),
            struct(2, count, *side),
            struct(2, count, *side),
            struct(2, count, win, win),
        ],
        compiler_params=params(),
        cost_estimate=cost(count * 7e9, count * 5e6),
    )(offs, obj, top, bot, lft, rgt, probe, amp, left, right)


def pack_kernel(near, far, top_near, top_far, bot_near, bot_far, left, right):
    tile = near.shape[2]
    mid = tile // 2
    for p in range(2):
        for refs, out, low in (
            ((top_near, near, bot_near), left, True),
            ((top_far, far, bot_far), right, False),
        ):
            body = refs[1][p, 0]
            upper = jnp.concatenate([refs[0][p, 0], body[:mid]], axis=0)
            lower = jnp.concatenate([body[mid:], refs[2][p, 0]], axis=0)
            lane = lax.broadcasted_iota(jnp.int32, upper.shape, 1)
            if low:
                out[p, 0] = jnp.where(lane < HALO, upper, pltpu.roll(lower, HALO, 1))
            else:
                out[p, 0] = jnp.where(lane < HALO, pltpu.roll(upper, HALO, 1), lower)


def pack_call(obj, top, bot, first, count):
    tile = obj.shape[2]
    last = tile // LANES - 1
    side = (tile // 2 + HALO, LANES)

    def lanes(rows, base, block):
        return pl.BlockSpec((2, 1, rows, LANES), lambda e: (0, base + e, 0, block))

    return pl.pallas_call(
        pack_kernel,
        grid=(count,),
        in_specs=[
            lanes(tile, first, 0),
            lanes(tile, first, last),
            lanes(HALO, 0, 0),
            lanes(HALO, 0, last),
            lanes(HALO, 0, 0),
            lanes(HALO, 0, last),
        ],
        out_specs=[plane(*side), plane(*side)],
        out_shape=[struct(2, count, *side)] * 2,
        compiler_params=params(),
        cost_estimate=cost(0, count * 12e5),
    )(obj, obj, top, top, bot, bot)


def from_left(packed, upper):
    lane = lax.broadcasted_iota(jnp.int32, packed.shape, 1)
    return jnp.where(lane < HALO, packed if upper else pltpu.roll(packed, HALO, 1), 0.0)


def from_right(packed, upper):
    lane = lax.broadcasted_iota(jnp.int32, packed.shape, 1)
    return jnp.where(lane < HALO, 0.0, pltpu.roll(packed, HALO, 1) if upper else packed)


def rim_kernel(g_top, g_bot, l_top, l_bot, r_top, r_bot, top, bot):
    for p in range(2):
        for g, l, r, out, upper in (
            (g_top, l_top, r_top, top, True),
            (g_bot, l_bot, r_bot, bot, False),
        ):
            out[p, 0] = g[p, 0]
            out[p, 0, :, :LANES] += from_left(l[p, 0], upper)
            out[p, 0, :, -LANES:] += from_right(r[p, 0], upper)


def rim_call(g, lft, rgt):
    count, rows, tile = g.shape[1:]

    def strip(block, width):
        return pl.BlockSpec((2, 1, HALO, width), lambda e: (0, e, block, 0))

    last = rows // HALO - 1
    packed_last = lft.shape[2] // HALO - 1
    return pl.pallas_call(
        rim_kernel,
        grid=(count,),
        in_specs=[
            strip(0, tile),
            strip(last, tile),
            strip(0, LANES),
            strip(packed_last, LANES),
            strip(0, LANES),
            strip(packed_last, LANES),
        ],
        out_specs=[plane(HALO, tile), plane(HALO, tile)],
        out_shape=[struct(2, count, HALO, tile)] * 2,
        compiler_params=params(),
        cost_estimate=cost(0, count * 8e5),
    )(g, g, lft, lft, rgt, rgt)


def step_kernel(obj, g, lft, rgt, above, below, out):
    tile = obj.shape[2]
    mid = tile // 2
    for p in range(2):
        l, r = lft[p, 0], rgt[p, 0]
        cols = (
            jnp.concatenate([from_left(l, True)[HALO:], from_left(l, False)[:mid]], axis=0),
            jnp.concatenate([from_right(r, True)[HALO:], from_right(r, False)[:mid]], axis=0),
        )
        for j, start in enumerate((0, tile - LANES)):
            span = slice(start, start + LANES)
            total = g[p, 0, HALO : HALO + tile, span] + cols[j]
            total = jnp.concatenate(
                [
                    total[:HALO] + above[p, 0, :, span],
                    total[HALO:-HALO],
                    total[-HALO:] + below[p, 0, :, span],
                ],
                axis=0,
            )
            out[p, 0, :, span] = obj[p, 0, :, span] - STEP * total


def step_call(obj, g, lft, rgt, above, below, first):
    tile = obj.shape[2]
    count, rows = g.shape[1:3]
    side = lft.shape[2:]
    return pl.pallas_call(
        step_kernel,
        grid=(count,),
        in_specs=[
            later(first, tile, tile),
            plane(rows, tile),
            plane(*side),
            plane(*side),
            plane(HALO, tile),
            plane(HALO, tile),
        ],
        out_specs=plane(tile, tile),
        out_shape=struct(2, count, tile, tile),
        compiler_params=params(),
        cost_estimate=cost(0, count * 25e5),
    )(obj, g, lft, rgt, above, below)


def probe_kernel(rate, probe, total, *rest):
    rest[-1][...] = probe[...] - rate * total[...]


def probe_call(probe, total, rate, first, running):
    win = probe.shape[2]
    count = total.shape[1]
    extra = [] if running is None else [running]
    return pl.pallas_call(
        lambda *refs: probe_kernel(rate, *refs),
        grid=(count,),
        in_specs=[later(first, win, win), plane(win, win)]
        + [pl.BlockSpec(memory_space=pl.ANY)] * len(extra),
        out_specs=later(first, win, win),
        out_shape=struct(*probe.shape),
        input_output_aliases={2: 0} if extra else {},
        compiler_params=params(),
        cost_estimate=cost(0, count * 16e5),
    )(probe, total, *extra)


def couple_kernel(weights, *refs):
    parts, out = refs[:-1], refs[-1]
    energies = out.shape[1]
    spans = chunks_of(energies)
    for g in range(out.shape[2] // SUB):
        rows = slice(g * SUB, (g + 1) * SUB)

        def flat(ref, q):
            x = ref[q, :, rows, :]
            return x.reshape(x.shape[0] * SUB, x.shape[2])

        own = [[flat(ref, q) for q in range(2)] for ref in parts[: len(spans)]]
        other = [[flat(ref, q) for q in range(2)] for ref in parts[len(spans) :]]
        hi, lo = split(jnp.concatenate([x for pair in own + other for x in pair], axis=0))
        mixed = dot(weights[...], jnp.concatenate([hi, lo, hi], axis=0))
        for (first, count), pair in zip(spans, own):
            for p in range(2):
                start = (p * energies + first) * SUB
                value = pair[p] + mixed[start : start + count * SUB]
                out[p, first : first + count, rows, :] = value.reshape(count, SUB, value.shape[1])


def couple_call(weights, parts, energies):
    tile = parts[0].shape[2]
    rows = 2 * SUB

    def block(count):
        return pl.BlockSpec((2, count, rows, tile), lambda i: (0, 0, i, 0))

    return pl.pallas_call(
        couple_kernel,
        grid=(tile // rows,),
        in_specs=[pl.BlockSpec(weights.shape, lambda i: (0, 0))]
        + [block(part.shape[1]) for part in parts],
        out_specs=block(energies),
        out_shape=struct(2, energies, tile, tile),
        compiler_params=params(),
        cost_estimate=cost(10e9, 26e6),
    )(weights, *parts)


def coupling_weights(kk_kernel, energies):
    count = lax.axis_size("energy")
    me = lax.axis_index("energy")
    mine = lax.dynamic_slice_in_dim(kk_kernel, me * energies, energies, axis=2)
    pieces = []
    for shift in range(count):
        source = (me - shift) % count
        block = lax.dynamic_slice_in_dim(mine, source * energies, energies, axis=3)
        block = block.transpose(0, 2, 1, 3)
        for first, size in chunks_of(energies):
            pieces.append(block[..., first : first + size].reshape(2 * energies, 2 * size))
    matrix = jnp.concatenate(pieces, axis=1)
    hi = lax.reduce_precision(matrix, 8, 7)
    matrix = jnp.concatenate([hi, hi, matrix - hi], axis=1)
    grown = matrix[:, None, :, None] * jnp.eye(SUB, dtype=jnp.float32)[None, :, None, :]
    return grown.reshape(matrix.shape[0] * SUB, matrix.shape[1] * SUB).astype(jnp.bfloat16)


def toward(block, axis, distance):
    count = lax.axis_size(axis)
    route = [(i, i + distance) for i in range(count) if 0 <= i + distance < count]
    return lax.ppermute(block, axis, route)


def local(object_field, probe_field, amplitudes, kk_kernel, offsets):
    energies = object_field.shape[1]
    ring = lax.axis_size("energy")
    tables = [jnp.asarray(m) for m in dft_parts(probe_field.shape[2])]
    offs = offsets.reshape(-1)
    weights = coupling_weights(kk_kernel, energies)
    rate = PROBE_STEP / (offsets.shape[2] * lax.axis_size("row") * lax.axis_size("col"))
    spans = chunks_of(energies)
    halos = []
    for first, count in spans:
        part = object_field[:, first : first + count]
        top = toward(part[:, :, -HALO:], "row", 1)
        bot = toward(part[:, :, :HALO], "row", -1)
        left, right = pack_call(object_field, top, bot, first, count)
        halos.append((top, bot, toward(right, "col", 1), toward(left, "col", -1)))
    own, other = [], [[] for _ in range(ring - 1)]
    new_probe = None
    totals = []
    for (first, count), halo in zip(spans, halos):
        g, g_left, g_right, probe_grad = gradient_call(
            offs, object_field, *halo, probe_field, amplitudes, *tables, first, count
        )
        totals.append(lax.psum(probe_grad, ("row", "col")))
        lft = toward(g_right, "col", 1)
        rgt = toward(g_left, "col", -1)
        top, bot = rim_call(g, lft, rgt)
        above = toward(bot, "row", 1)
        below = toward(top, "row", -1)
        stepped = step_call(object_field, g, lft, rgt, above, below, first)
        own.append(stepped)
        for shift in range(1, ring):
            route = [(i, (i + shift) % ring) for i in range(ring)]
            other[shift - 1].append(lax.ppermute(stepped, "energy", route))
    for (first, count), total in zip(spans, totals):
        new_probe = probe_call(probe_field, total, rate, first, new_probe)
    blended = couple_call(weights, own + [x for group in other for x in group], energies)
    return (blended, new_probe)


def solution(mesh):
    return jax.shard_map(
        local,
        mesh=mesh,
        in_specs=(
            P(None, "energy", "row", "col"),
            P(None, "energy", None, None),
            P("energy", "row", "col", None, None, None),
            P(),
            P("row", "col", None, None),
        ),
        out_specs=(P(None, "energy", "row", "col"), P(None, "energy", None, None)),
        check_vma=False,
    )
```

```python
import math

import jax
import jax.numpy as jnp
import ml_dtypes
import numpy as np
from jax import lax
from jax.experimental import pallas as pl
from jax.experimental.pallas import tpu as pltpu
from jax.sharding import PartitionSpec as P

HALO = 64
LANES = 128
SUB = 8
STEP = 0.25
PROBE_STEP = 0.5
FLOOR = 0.25
PARTS = (3, 7, 6)
VMEM = 56 * 2**20


def chunks_of(energies):
    if energies == sum(PARTS):
        sizes = PARTS
    else:
        sizes = (1,) * energies
    return [(sum(sizes[:i]), size) for i, size in enumerate(sizes)]


def split(x):
    hi = x.astype(jnp.bfloat16)
    return hi, (x - hi.astype(jnp.float32)).astype(jnp.bfloat16)


def dft_parts(length):
    half = length // 2
    pixel = np.arange(half)
    even = pixel - pixel % 2 + half * (pixel % 2)
    out = []
    for freqs in (even, even + 1):
        angle = (freqs[:, None] * pixel[None, :] % length) * (2.0 * math.pi / length)
        c, s = np.cos(angle) / math.sqrt(length), np.sin(angle) / math.sqrt(length)
        m = np.block([[c, s], [-s, c]])
        hi = m.astype(np.float32).astype(ml_dtypes.bfloat16)
        lo = (m - hi.astype(np.float64)).astype(np.float32).astype(ml_dtypes.bfloat16)
        out.append((hi, lo))
    even, odd = out
    wide = lambda m: np.concatenate([m[0], m[0], m[1]], axis=1)
    tall = lambda m: np.concatenate([m[0], m[0], m[1]], axis=0)
    t = lambda m: (m[0].T, m[1].T)
    left = np.stack([wide(even), wide(odd), wide(t(even)), wide(t(odd))])
    right = np.stack([tall(t(even)), tall(t(odd)), tall(even), tall(odd)])
    return left, right


def dot(a, b):
    return jnp.dot(a, b, preferred_element_type=jnp.float32)


def gradient_kernel(
    tiles, rate, offs, obj, top, bot, lft, rgt, probe, amp, left, right, gout, gl, gr, pg, ext, grad
):
    win = probe.shape[2]
    tile = obj.shape[2]
    half = win // 2
    rows = tile + 2 * HALO
    mid = rows // 2
    lane = lax.broadcasted_iota(jnp.int32, (win, LANES), 1)
    for p in range(2):
        for j in range(tile // LANES):
            cols = slice(j * LANES, (j + 1) * LANES)
            ext[p, 1 + j, 0:HALO] = top[p, 0, :, cols]
            ext[p, 1 + j, HALO : HALO + tile] = obj[p, 0, :, cols]
            ext[p, 1 + j, HALO + tile : rows] = bot[p, 0, :, cols]
        packed = lft[p, 0]
        ext[p, 0, 0:mid] = pltpu.roll(packed, HALO, 1)
        ext[p, 0, mid:rows] = packed
        packed = rgt[p, 0]
        ext[p, 3, 0:mid] = packed
        ext[p, 3, mid:rows] = pltpu.roll(packed, HALO, 1)
    grad[...] = jnp.zeros_like(grad)
    pg[...] = jnp.zeros_like(pg)

    def window_of(k):
        a = offs[2 * k]
        b = offs[2 * k + 1] + HALO
        base = b // LANES
        r = b % LANES
        back = (LANES - r) % LANES
        return a, base, r, back

    def position(k):
        a, base, r, back = window_of(k)
        keep = lane < LANES - r
        def load(p):
            v = [pltpu.roll(ext[p, base + j, pl.ds(a, win), :], back, 1) for j in range(3)]
            return jnp.concatenate([jnp.where(keep, v[0], v[1]), jnp.where(keep, v[1], v[2])], axis=1)
        wr, wi = load(0), load(1)
        pr, pi = probe[0, 0], probe[1, 0]
        er = pr * wr - pi * wi
        ei = pr * wi + pi * wr

        def lmul(which, top_, bottom_):
            hi, lo = split(jnp.concatenate([top_, bottom_], axis=0))
            return dot(left[which], jnp.concatenate([hi, lo, hi], axis=0))

        def rmul(which, l_, r_):
            hi, lo = split(jnp.concatenate([l_, r_], axis=1))
            return dot(jnp.concatenate([hi, lo, hi], axis=1), right[which])

        ze = lmul(0, er[:half] + er[half:], ei[:half] + ei[half:])
        zo = lmul(1, er[:half] - er[half:], ei[:half] - ei[half:])
        zr = jnp.concatenate([ze[:half], zo[:half]], axis=0)
        zi = jnp.concatenate([ze[half:], zo[half:]], axis=0)
        ye = rmul(0, zr[:, :half] + zr[:, half:], zi[:, :half] + zi[:, half:])
        yo = rmul(1, zr[:, :half] - zr[:, half:], zi[:, :half] - zi[:, half:])
        meas = amp[0, 0, 0, k]
        groups = (half // 8, 8, win)
        mt, mb = meas[:half].reshape(groups), meas[half:].reshape(groups)
        odd_row = lax.broadcasted_iota(jnp.int32, groups, 1) % 2 == 1
        meas = jnp.concatenate(
            [
                jnp.where(odd_row, pltpu.roll(mb, 1, 1), mt).reshape(half, win),
                jnp.where(odd_row, mb, pltpu.roll(mt, 7, 1)).reshape(half, win),
            ],
            axis=0,
        )
        odd = lane % 2 == 1
        ml, mr = meas[:, :half], meas[:, half:]
        me = jnp.where(odd, pltpu.roll(mr, 1, 1), ml)
        mo = jnp.where(odd, mr, pltpu.roll(ml, LANES - 1, 1))

        def fix(y, m_):
            fr, fi = y[:, :half], y[:, half:]
            s = m_ * lax.rsqrt(jnp.maximum(fr * fr + fi * fi, FLOOR * FLOOR))
            return fr * s, fi * s

        te = rmul(2, *fix(ye, me))
        to = rmul(3, *fix(yo, mo))
        sr, dr = te[:, :half] + to[:, :half], te[:, :half] - to[:, :half]
        si, di = te[:, half:] + to[:, half:], te[:, half:] - to[:, half:]
        xr = jnp.concatenate([sr, dr], axis=1)
        xi = jnp.concatenate([si, di], axis=1)
        be = lmul(2, xr[:half], xi[:half])
        bo = lmul(3, xr[half:], xi[half:])
        br = jnp.concatenate([be[:half] + bo[:half], be[:half] - bo[:half]], axis=0)
        bi = jnp.concatenate([be[half:] + bo[half:], be[half:] - bo[half:]], axis=0)
        dr, di = er - br, ei - bi
        pg[0, 0] += wr * dr + wi * di
        pg[1, 0] += wr * di - wi * dr
        steps = (pr * dr + pi * di, pr * di - pi * dr)
        below = lane < r
        for p in range(2):
            u = pltpu.roll(steps[p][:, :LANES], r, 1)
            v = pltpu.roll(steps[p][:, LANES:], r, 1)
            grad[p, base, pl.ds(a, win), :] += jnp.where(below, 0.0, u)
            grad[p, base + 1, pl.ds(a, win), :] += jnp.where(below, u, v)
            grad[p, base + 2, pl.ds(a, win), :] += jnp.where(below, v, 0.0)

    for k in range(amp.shape[3]):
        position(k)
    pg[...] = probe[...] * (1.0 / tiles) - rate * pg[...]
    first = lax.broadcasted_iota(jnp.int32, (mid, LANES), 1) < HALO
    for p in range(2):
        for j in range(tile // LANES):
            gout[p, 0, :, j * LANES : (j + 1) * LANES] = grad[p, 1 + j]
        edge = grad.at[p, 0]
        gl[p, 0] = jnp.where(first, pltpu.roll(edge[0:mid], HALO, 1), edge[mid:rows])
        edge = grad.at[p, 3]
        gr[p, 0] = jnp.where(first, edge[0:mid], pltpu.roll(edge[mid:rows], HALO, 1))


def params():
    return pltpu.CompilerParams(vmem_limit_bytes=VMEM)


def cost(flops, moved):
    return pl.CostEstimate(flops=int(flops), bytes_accessed=int(moved), transcendentals=0)


def anywhere(arrays):
    return [pl.BlockSpec(memory_space=pl.ANY)] * len(arrays)


def ordered(kernel, inputs, after):
    def body(*refs):
        return kernel(*refs[:inputs], *refs[inputs + len(after) :])

    return body


def plane(*shape):
    return pl.BlockSpec((2, 1) + shape, lambda e, *_: (0, e, 0, 0))


def later(first, *shape):
    return pl.BlockSpec((2, 1) + shape, lambda e, *_: (0, first + e, 0, 0))


def struct(*shape):
    return jax.ShapeDtypeStruct(shape, jnp.float32)


def gradient_call(
    scales, offs, obj, top, bot, lft, rgt, probe, amp, left, right, first, count, running, after
):
    win, tile = probe.shape[2], obj.shape[2]
    rows = tile + 2 * HALO
    side = (rows // 2, LANES)
    frame = pltpu.VMEM((2, tile // LANES + 2, rows, LANES), jnp.float32)
    whole = lambda m: pl.BlockSpec(m.shape, lambda e, *_: (0, 0, 0))
    return pl.pallas_call(
        ordered(lambda *refs: gradient_kernel(*scales, *refs), 10, running + after),
        grid_spec=pltpu.PrefetchScalarGridSpec(
            num_scalar_prefetch=1,
            grid=(count,),
            in_specs=[
                later(first, tile, tile),
                plane(HALO, tile),
                plane(HALO, tile),
                plane(*side),
                plane(*side),
                later(first, win, win),
                pl.BlockSpec((1, 1, 1) + amp.shape[3:], lambda e, *_: (first + e, 0, 0, 0, 0, 0)),
                whole(left),
                whole(right),
            ]
            + anywhere(running + after),
            out_specs=[plane(rows, tile), plane(*side), plane(*side), later(first, win, win)],
            scratch_shapes=[frame, frame],
        ),
        out_shape=[
            struct(2, count, rows, tile),
            struct(2, count, *side),
            struct(2, count, *side),
            struct(*probe.shape),
        ],
        input_output_aliases={10: 3} if running else {},
        compiler_params=params(),
        cost_estimate=cost(count * 7e9, count * 5e6),
    )(offs, obj, top, bot, lft, rgt, probe, amp, left, right, *running, *after)


def pack_kernel(near, far, top_near, top_far, bot_near, bot_far, left, right):
    tile = near.shape[2]
    mid = tile // 2
    for p in range(2):
        for refs, out, low in (
            ((top_near, near, bot_near), left, True),
            ((top_far, far, bot_far), right, False),
        ):
            body = refs[1][p, 0]
            upper = jnp.concatenate([refs[0][p, 0], body[:mid]], axis=0)
            lower = jnp.concatenate([body[mid:], refs[2][p, 0]], axis=0)
            lane = lax.broadcasted_iota(jnp.int32, upper.shape, 1)
            if low:
                out[p, 0] = jnp.where(lane < HALO, upper, pltpu.roll(lower, HALO, 1))
            else:
                out[p, 0] = jnp.where(lane < HALO, pltpu.roll(upper, HALO, 1), lower)


def pack_call(obj, top, bot, first, count, after):
    tile = obj.shape[2]
    last = tile // LANES - 1
    side = (tile // 2 + HALO, LANES)

    def lanes(rows, base, block):
        return pl.BlockSpec((2, 1, rows, LANES), lambda e: (0, base + e, 0, block))

    return pl.pallas_call(
        ordered(pack_kernel, 6, after),
        grid=(count,),
        in_specs=[
            lanes(tile, first, 0),
            lanes(tile, first, last),
            lanes(HALO, 0, 0),
            lanes(HALO, 0, last),
            lanes(HALO, 0, 0),
            lanes(HALO, 0, last),
        ]
        + anywhere(after),
        out_specs=[plane(*side), plane(*side)],
        out_shape=[struct(2, count, *side)] * 2,
        compiler_params=params(),
        cost_estimate=cost(0, count * 12e5),
    )(obj, obj, top, top, bot, bot, *after)


def from_left(packed, upper):
    lane = lax.broadcasted_iota(jnp.int32, packed.shape, 1)
    return jnp.where(lane < HALO, packed if upper else pltpu.roll(packed, HALO, 1), 0.0)


def from_right(packed, upper):
    lane = lax.broadcasted_iota(jnp.int32, packed.shape, 1)
    return jnp.where(lane < HALO, 0.0, pltpu.roll(packed, HALO, 1) if upper else packed)


def rim_kernel(g_top, g_bot, l_top, l_bot, r_top, r_bot, top, bot):
    for p in range(2):
        for g, l, r, out, upper in (
            (g_top, l_top, r_top, top, True),
            (g_bot, l_bot, r_bot, bot, False),
        ):
            out[p, 0] = g[p, 0]
            out[p, 0, :, :LANES] += from_left(l[p, 0], upper)
            out[p, 0, :, -LANES:] += from_right(r[p, 0], upper)


def rim_call(g, lft, rgt, after):
    count, rows, tile = g.shape[1:]

    def strip(block, width):
        return pl.BlockSpec((2, 1, HALO, width), lambda e: (0, e, block, 0))

    last = rows // HALO - 1
    packed_last = lft.shape[2] // HALO - 1
    return pl.pallas_call(
        ordered(rim_kernel, 6, after),
        grid=(count,),
        in_specs=[
            strip(0, tile),
            strip(last, tile),
            strip(0, LANES),
            strip(packed_last, LANES),
            strip(0, LANES),
            strip(packed_last, LANES),
        ]
        + anywhere(after),
        out_specs=[plane(HALO, tile), plane(HALO, tile)],
        out_shape=[struct(2, count, HALO, tile)] * 2,
        compiler_params=params(),
        cost_estimate=cost(1e3, 1e3),
    )(g, g, lft, lft, rgt, rgt, *after)


def step_kernel(obj, g, lft, rgt, above, below, out):
    tile = obj.shape[2]
    mid = tile // 2
    for p in range(2):
        l, r = lft[p, 0], rgt[p, 0]
        cols = (
            jnp.concatenate([from_left(l, True)[HALO:], from_left(l, False)[:mid]], axis=0),
            jnp.concatenate([from_right(r, True)[HALO:], from_right(r, False)[:mid]], axis=0),
        )
        for j, start in enumerate((0, tile - LANES)):
            span = slice(start, start + LANES)
            total = g[p, 0, HALO : HALO + tile, span] + cols[j]
            total = jnp.concatenate(
                [
                    total[:HALO] + above[p, 0, :, span],
                    total[HALO:-HALO],
                    total[-HALO:] + below[p, 0, :, span],
                ],
                axis=0,
            )
            out[p, 0, :, span] = obj[p, 0, :, span] - STEP * total


def step_call(obj, g, lft, rgt, above, below, first, after):
    tile = obj.shape[2]
    count, rows = g.shape[1:3]
    side = lft.shape[2:]
    return pl.pallas_call(
        ordered(step_kernel, 6, after),
        grid=(count,),
        in_specs=[
            later(first, tile, tile),
            plane(rows, tile),
            plane(*side),
            plane(*side),
            plane(HALO, tile),
            plane(HALO, tile),
        ]
        + anywhere(after),
        out_specs=plane(tile, tile),
        out_shape=struct(2, count, tile, tile),
        compiler_params=params(),
        cost_estimate=cost(1e3, 1e3),
    )(obj, g, lft, rgt, above, below, *after)


def couple_kernel(table, choose, *refs):
    parts, out, weights = refs[:-2], refs[-2], refs[-1]
    energies = out.shape[1]
    spans = chunks_of(energies)
    width = choose.shape[1]

    @pl.when(pl.program_id(0) == 0)
    def _():
        rows = lax.broadcasted_iota(jnp.int32, (weights.shape[0], table.shape[0]), 0)
        source = lax.broadcasted_iota(jnp.int32, rows.shape, 1)
        spread = (rows // SUB == source).astype(jnp.bfloat16)
        wide = (weights.shape[0], width)
        lane = lax.broadcasted_iota(jnp.int32, wide, 1)
        same = lax.broadcasted_iota(jnp.int32, wide, 0) % SUB == lane % SUB
        for part, spots in zip(split(table[...]), ((0, 1), (2,))):
            picked = dot(part, choose[...]).astype(jnp.bfloat16)
            grown = jnp.where(same, dot(spread, picked), 0.0).astype(jnp.bfloat16)
            for spot in spots:
                weights[:, spot * width : (spot + 1) * width] = grown

    for g in range(out.shape[2] // SUB):
        rows = slice(g * SUB, (g + 1) * SUB)

        def flat(ref, q):
            x = ref[q, :, rows, :]
            return x.reshape(x.shape[0] * SUB, x.shape[2])

        own = [[flat(ref, q) for q in range(2)] for ref in parts[: len(spans)]]
        other = [[flat(ref, q) for q in range(2)] for ref in parts[len(spans) :]]
        hi, lo = split(jnp.concatenate([x for pair in own + other for x in pair], axis=0))
        mixed = dot(weights[...], jnp.concatenate([hi, lo, hi], axis=0))
        for (first, count), pair in zip(spans, own):
            for p in range(2):
                start = (p * energies + first) * SUB
                value = pair[p] + mixed[start : start + count * SUB]
                out[p, first : first + count, rows, :] = value.reshape(count, SUB, value.shape[1])


def couple_call(table, choose, parts, energies, after):
    tile = parts[0].shape[2]
    rows = 2 * SUB

    def block(count):
        return pl.BlockSpec((2, count, rows, tile), lambda i: (0, 0, i, 0))

    return pl.pallas_call(
        ordered(couple_kernel, 2 + len(parts), after),
        grid=(tile // rows,),
        in_specs=[
            pl.BlockSpec(table.shape, lambda i: (0, 0)),
            pl.BlockSpec(choose.shape, lambda i: (0, 0)),
        ]
        + [block(part.shape[1]) for part in parts]
        + anywhere(after),
        out_specs=block(energies),
        out_shape=struct(2, energies, tile, tile),
        scratch_shapes=[pltpu.VMEM((2 * energies * SUB, 3 * choose.shape[1]), jnp.bfloat16)],
        compiler_params=params(),
        cost_estimate=cost(1e3, 1e3),
    )(table, choose, *parts, *after)


def coupling(kk_kernel, energies):
    count = lax.axis_size("energy")
    me = lax.axis_index("energy")
    total = kk_kernel.shape[3]
    mine = lax.dynamic_slice_in_dim(kk_kernel, me * energies, energies, axis=2)
    table = mine.transpose(0, 2, 1, 3).reshape(2 * energies, 2 * total)
    shift, within, base = [], [], []
    for step in range(count):
        for first, size in chunks_of(energies):
            for q in range(2):
                for f in range(first, first + size):
                    shift += [step] * SUB
                    within += [f] * SUB
                    base += [q * total] * SUB
    source = (me - jnp.asarray(shift, jnp.int32)) % count
    column = jnp.asarray(base, jnp.int32) + source * energies + jnp.asarray(within, jnp.int32)
    row = lax.broadcasted_iota(jnp.int32, (2 * total, len(shift)), 0)
    return table, (row == column[None]).astype(jnp.bfloat16)


def toward(block, axis, distance):
    count = lax.axis_size(axis)
    route = [(i, i + distance) for i in range(count) if 0 <= i + distance < count]
    return lax.ppermute(block, axis, route)


def local(object_field, probe_field, amplitudes, kk_kernel, offsets):
    energies = object_field.shape[1]
    ring = lax.axis_size("energy")
    tables = [jnp.asarray(m) for m in dft_parts(probe_field.shape[2])]
    offs = offsets.reshape(-1)
    table, choose = coupling(kk_kernel, energies)
    tiles = lax.axis_size("row") * lax.axis_size("col")
    scales = (tiles, PROBE_STEP / (offsets.shape[2] * tiles))
    spans = chunks_of(energies)
    energy_route = lambda shift: [(i, (i + shift) % ring) for i in range(ring)]
    halos, grads, own = [], [], []
    other = [[] for _ in range(ring - 1)]
    for first, count in spans:
        part = object_field[:, first : first + count]
        top, bot = toward(part[:, :, -HALO:], "row", 1), toward(part[:, :, :HALO], "row", -1)
        left, right = pack_call(object_field, top, bot, first, count, [])
        halos.append((top, bot, toward(right, "col", 1), toward(left, "col", -1)))
    rims = []

    def trim(i):
        g, g_left, g_right = grads[i]
        lft = toward(g_right, "col", 1)
        rgt = toward(g_left, "col", -1)
        top, bot = rim_call(g, lft, rgt, [])
        rims.append((g, lft, rgt, toward(bot, "row", 1), toward(top, "row", -1)))
        return top

    running, after = [], []
    for i, ((first, count), halo) in enumerate(zip(spans, halos)):
        *grad, share = gradient_call(
            scales, offs, object_field, *halo, probe_field, amplitudes, *tables,
            first, count, running, after,
        )
        grads.append(grad)
        running, after = [share], []
        if i == len(spans) - 2:
            after = [trim(len(rims))]
    new_probe = lax.psum(share, ("row", "col"))
    for i, (first, count) in enumerate(spans):
        if i >= len(rims):
            trim(i)
        after = own[-1:]
        if i == len(spans) - 1:
            after = after + [group[0] for group in other]
        own.append(step_call(object_field, *rims[i], first, after))
        for shift in range(1, ring):
            other[shift - 1].append(lax.ppermute(own[-1], "energy", energy_route(shift)))
    other = [x for group in other for x in group]
    blended = couple_call(table, choose, own + other, energies, [])
    return (blended, new_probe)


def solution(mesh):
    return jax.shard_map(
        local,
        mesh=mesh,
        in_specs=(
            P(None, "energy", "row", "col"),
            P(None, "energy", None, None),
            P("energy", "row", "col", None, None, None),
            P(),
            P("row", "col", None, None),
        ),
        out_specs=(P(None, "energy", "row", "col"), P(None, "energy", None, None)),
        check_vma=False,
    )
```

```python
import math

import jax
import jax.numpy as jnp
import ml_dtypes
import numpy as np
from jax import lax
from jax.experimental import pallas as pl
from jax.experimental.pallas import tpu as pltpu
from jax.sharding import PartitionSpec as P

HALO = 64
LANES = 128
SUB = 8
STEP = 0.25
PROBE_STEP = 0.5
FLOOR = 0.25
PARTS = (5, 6, 5)
VMEM = 56 * 2**20


def chunks_of(energies):
    if energies == sum(PARTS):
        sizes = PARTS
    else:
        sizes = (1,) * energies
    return [(sum(sizes[:i]), size) for i, size in enumerate(sizes)]


def split(x):
    hi = x.astype(jnp.bfloat16)
    return hi, (x - hi.astype(jnp.float32)).astype(jnp.bfloat16)


def dft_parts(length):
    half = length // 2
    pixel = np.arange(half)
    even = pixel - pixel % 2 + half * (pixel % 2)
    out = []
    for freqs in (even, even + 1):
        angle = (freqs[:, None] * pixel[None, :] % length) * (2.0 * math.pi / length)
        c, s = np.cos(angle) / math.sqrt(length), np.sin(angle) / math.sqrt(length)
        m = np.block([[c, s], [-s, c]])
        hi = m.astype(np.float32).astype(ml_dtypes.bfloat16)
        lo = (m - hi.astype(np.float64)).astype(np.float32).astype(ml_dtypes.bfloat16)
        out.append((hi, lo))
    even, odd = out
    wide = lambda m: np.concatenate([m[0], m[0], m[1]], axis=1)
    tall = lambda m: np.concatenate([m[0], m[0], m[1]], axis=0)
    t = lambda m: (m[0].T, m[1].T)
    left = np.stack([wide(even), wide(odd), wide(t(even)), wide(t(odd))])
    right = np.stack([tall(t(even)), tall(t(odd)), tall(even), tall(odd)])
    return left, right


def dot(a, b):
    return jnp.dot(a, b, preferred_element_type=jnp.float32)


def gradient_kernel(
    tiles, rate, offs, obj, top, bot, lft, rgt, probe, amp, left, right, gout, gl, gr, pg, ext, grad
):
    win = probe.shape[2]
    tile = obj.shape[2]
    half = win // 2
    rows = tile + 2 * HALO
    mid = rows // 2
    lane = lax.broadcasted_iota(jnp.int32, (win, LANES), 1)
    for p in range(2):
        for j in range(tile // LANES):
            cols = slice(j * LANES, (j + 1) * LANES)
            ext[p, 1 + j, 0:HALO] = top[p, 0, :, cols]
            ext[p, 1 + j, HALO : HALO + tile] = obj[p, 0, :, cols]
            ext[p, 1 + j, HALO + tile : rows] = bot[p, 0, :, cols]
        packed = lft[p, 0]
        ext[p, 0, 0:mid] = pltpu.roll(packed, HALO, 1)
        ext[p, 0, mid:rows] = packed
        packed = rgt[p, 0]
        ext[p, 3, 0:mid] = packed
        ext[p, 3, mid:rows] = pltpu.roll(packed, HALO, 1)
    grad[...] = jnp.zeros_like(grad)
    pg[...] = jnp.zeros_like(pg)

    def window_of(k):
        a = offs[2 * k]
        b = offs[2 * k + 1] + HALO
        base = b // LANES
        r = b % LANES
        back = (LANES - r) % LANES
        return a, base, r, back

    def position(k):
        a, base, r, back = window_of(k)
        keep = lane < LANES - r
        def load(p):
            v = [pltpu.roll(ext[p, base + j, pl.ds(a, win), :], back, 1) for j in range(3)]
            return jnp.concatenate([jnp.where(keep, v[0], v[1]), jnp.where(keep, v[1], v[2])], axis=1)
        wr, wi = load(0), load(1)
        pr, pi = probe[0, 0], probe[1, 0]
        er = pr * wr - pi * wi
        ei = pr * wi + pi * wr

        def lmul(which, top_, bottom_):
            hi, lo = split(jnp.concatenate([top_, bottom_], axis=0))
            return dot(left[which], jnp.concatenate([hi, lo, hi], axis=0))

        def rmul(which, l_, r_):
            hi, lo = split(jnp.concatenate([l_, r_], axis=1))
            return dot(jnp.concatenate([hi, lo, hi], axis=1), right[which])

        ze = lmul(0, er[:half] + er[half:], ei[:half] + ei[half:])
        zo = lmul(1, er[:half] - er[half:], ei[:half] - ei[half:])
        zr = jnp.concatenate([ze[:half], zo[:half]], axis=0)
        zi = jnp.concatenate([ze[half:], zo[half:]], axis=0)
        ye = rmul(0, zr[:, :half] + zr[:, half:], zi[:, :half] + zi[:, half:])
        yo = rmul(1, zr[:, :half] - zr[:, half:], zi[:, :half] - zi[:, half:])
        meas = amp[0, 0, 0, k]
        groups = (half // 8, 8, win)
        mt, mb = meas[:half].reshape(groups), meas[half:].reshape(groups)
        odd_row = lax.broadcasted_iota(jnp.int32, groups, 1) % 2 == 1
        meas = jnp.concatenate(
            [
                jnp.where(odd_row, pltpu.roll(mb, 1, 1), mt).reshape(half, win),
                jnp.where(odd_row, mb, pltpu.roll(mt, 7, 1)).reshape(half, win),
            ],
            axis=0,
        )
        odd = lane % 2 == 1
        ml, mr = meas[:, :half], meas[:, half:]
        me = jnp.where(odd, pltpu.roll(mr, 1, 1), ml)
        mo = jnp.where(odd, mr, pltpu.roll(ml, LANES - 1, 1))

        def fix(y, m_):
            fr, fi = y[:, :half], y[:, half:]
            s = m_ * lax.rsqrt(jnp.maximum(fr * fr + fi * fi, FLOOR * FLOOR))
            return fr * s, fi * s

        te = rmul(2, *fix(ye, me))
        to = rmul(3, *fix(yo, mo))
        sr, dr = te[:, :half] + to[:, :half], te[:, :half] - to[:, :half]
        si, di = te[:, half:] + to[:, half:], te[:, half:] - to[:, half:]
        xr = jnp.concatenate([sr, dr], axis=1)
        xi = jnp.concatenate([si, di], axis=1)
        be = lmul(2, xr[:half], xi[:half])
        bo = lmul(3, xr[half:], xi[half:])
        br = jnp.concatenate([be[:half] + bo[:half], be[:half] - bo[:half]], axis=0)
        bi = jnp.concatenate([be[half:] + bo[half:], be[half:] - bo[half:]], axis=0)
        dr, di = er - br, ei - bi
        pg[0, 0] += wr * dr + wi * di
        pg[1, 0] += wr * di - wi * dr
        steps = (pr * dr + pi * di, pr * di - pi * dr)
        below = lane < r
        for p in range(2):
            u = pltpu.roll(steps[p][:, :LANES], r, 1)
            v = pltpu.roll(steps[p][:, LANES:], r, 1)
            grad[p, base, pl.ds(a, win), :] += jnp.where(below, 0.0, u)
            grad[p, base + 1, pl.ds(a, win), :] += jnp.where(below, u, v)
            grad[p, base + 2, pl.ds(a, win), :] += jnp.where(below, v, 0.0)

    for k in range(amp.shape[3]):
        position(k)
    pg[...] = probe[...] * (1.0 / tiles) - rate * pg[...]
    first = lax.broadcasted_iota(jnp.int32, (mid, LANES), 1) < HALO
    for p in range(2):
        for j in range(tile // LANES):
            gout[p, 0, :, j * LANES : (j + 1) * LANES] = grad[p, 1 + j]
        edge = grad.at[p, 0]
        gl[p, 0] = jnp.where(first, pltpu.roll(edge[0:mid], HALO, 1), edge[mid:rows])
        edge = grad.at[p, 3]
        gr[p, 0] = jnp.where(first, edge[0:mid], pltpu.roll(edge[mid:rows], HALO, 1))


def params():
    return pltpu.CompilerParams(vmem_limit_bytes=VMEM)


def cost(flops, moved):
    return pl.CostEstimate(flops=1000, bytes_accessed=1000, transcendentals=0)


def anywhere(arrays):
    return [pl.BlockSpec(memory_space=pl.ANY)] * len(arrays)


def ordered(kernel, inputs, after):
    def body(*refs):
        return kernel(*refs[:inputs], *refs[inputs + len(after) :])

    return body


def plane(*shape):
    return pl.BlockSpec((2, 1) + shape, lambda e, *_: (0, e, 0, 0))


def later(first, *shape):
    return pl.BlockSpec((2, 1) + shape, lambda e, *_: (0, first + e, 0, 0))


def struct(*shape):
    return jax.ShapeDtypeStruct(shape, jnp.float32)


def gradient_call(
    scales, offs, obj, top, bot, lft, rgt, probe, amp, left, right, first, count, running, after
):
    win, tile = probe.shape[2], obj.shape[2]
    rows = tile + 2 * HALO
    side = (rows // 2, LANES)
    frame = pltpu.VMEM((2, tile // LANES + 2, rows, LANES), jnp.float32)
    whole = lambda m: pl.BlockSpec(m.shape, lambda e, *_: (0, 0, 0))
    return pl.pallas_call(
        ordered(lambda *refs: gradient_kernel(*scales, *refs), 10, running + after),
        grid_spec=pltpu.PrefetchScalarGridSpec(
            num_scalar_prefetch=1,
            grid=(count,),
            in_specs=[
                later(first, tile, tile),
                plane(HALO, tile),
                plane(HALO, tile),
                plane(*side),
                plane(*side),
                later(first, win, win),
                pl.BlockSpec((1, 1, 1) + amp.shape[3:], lambda e, *_: (first + e, 0, 0, 0, 0, 0)),
                whole(left),
                whole(right),
            ]
            + anywhere(running + after),
            out_specs=[plane(rows, tile), plane(*side), plane(*side), later(first, win, win)],
            scratch_shapes=[frame, frame],
        ),
        out_shape=[
            struct(2, count, rows, tile),
            struct(2, count, *side),
            struct(2, count, *side),
            struct(*probe.shape),
        ],
        input_output_aliases={10: 3} if running else {},
        compiler_params=params(),
        cost_estimate=cost(count * 7e9, count * 5e6),
    )(offs, obj, top, bot, lft, rgt, probe, amp, left, right, *running, *after)


def pack_kernel(near, far, top_near, top_far, bot_near, bot_far, left, right):
    tile = near.shape[2]
    mid = tile // 2
    for p in range(2):
        for refs, out, low in (
            ((top_near, near, bot_near), left, True),
            ((top_far, far, bot_far), right, False),
        ):
            body = refs[1][p, 0]
            upper = jnp.concatenate([refs[0][p, 0], body[:mid]], axis=0)
            lower = jnp.concatenate([body[mid:], refs[2][p, 0]], axis=0)
            lane = lax.broadcasted_iota(jnp.int32, upper.shape, 1)
            if low:
                out[p, 0] = jnp.where(lane < HALO, upper, pltpu.roll(lower, HALO, 1))
            else:
                out[p, 0] = jnp.where(lane < HALO, pltpu.roll(upper, HALO, 1), lower)


def pack_call(obj, top, bot, first, count, after):
    tile = obj.shape[2]
    last = tile // LANES - 1
    side = (tile // 2 + HALO, LANES)

    def lanes(rows, base, block):
        return pl.BlockSpec((2, 1, rows, LANES), lambda e: (0, base + e, 0, block))

    return pl.pallas_call(
        ordered(pack_kernel, 6, after),
        grid=(count,),
        in_specs=[
            lanes(tile, first, 0),
            lanes(tile, first, last),
            lanes(HALO, 0, 0),
            lanes(HALO, 0, last),
            lanes(HALO, 0, 0),
            lanes(HALO, 0, last),
        ]
        + anywhere(after),
        out_specs=[plane(*side), plane(*side)],
        out_shape=[struct(2, count, *side)] * 2,
        compiler_params=params(),
        cost_estimate=cost(0, count * 12e5),
    )(obj, obj, top, top, bot, bot, *after)


def from_left(packed, upper):
    lane = lax.broadcasted_iota(jnp.int32, packed.shape, 1)
    return jnp.where(lane < HALO, packed if upper else pltpu.roll(packed, HALO, 1), 0.0)


def from_right(packed, upper):
    lane = lax.broadcasted_iota(jnp.int32, packed.shape, 1)
    return jnp.where(lane < HALO, 0.0, pltpu.roll(packed, HALO, 1) if upper else packed)


def rim_kernel(g_top, g_bot, l_top, l_bot, r_top, r_bot, top, bot):
    for p in range(2):
        for g, l, r, out, upper in (
            (g_top, l_top, r_top, top, True),
            (g_bot, l_bot, r_bot, bot, False),
        ):
            out[p, 0] = g[p, 0]
            out[p, 0, :, :LANES] += from_left(l[p, 0], upper)
            out[p, 0, :, -LANES:] += from_right(r[p, 0], upper)


def rim_call(g, lft, rgt, after):
    count, rows, tile = g.shape[1:]

    def strip(block, width):
        return pl.BlockSpec((2, 1, HALO, width), lambda e: (0, e, block, 0))

    last = rows // HALO - 1
    packed_last = lft.shape[2] // HALO - 1
    return pl.pallas_call(
        ordered(rim_kernel, 6, after),
        grid=(count,),
        in_specs=[
            strip(0, tile),
            strip(last, tile),
            strip(0, LANES),
            strip(packed_last, LANES),
            strip(0, LANES),
            strip(packed_last, LANES),
        ]
        + anywhere(after),
        out_specs=[plane(HALO, tile), plane(HALO, tile)],
        out_shape=[struct(2, count, HALO, tile)] * 2,
        compiler_params=params(),
        cost_estimate=cost(1e3, 1e3),
    )(g, g, lft, lft, rgt, rgt, *after)


def step_kernel(obj, g, lft, rgt, above, below, out):
    tile = obj.shape[2]
    mid = tile // 2
    for p in range(2):
        l, r = lft[p, 0], rgt[p, 0]
        cols = (
            jnp.concatenate([from_left(l, True)[HALO:], from_left(l, False)[:mid]], axis=0),
            jnp.concatenate([from_right(r, True)[HALO:], from_right(r, False)[:mid]], axis=0),
        )
        for j, start in enumerate((0, tile - LANES)):
            span = slice(start, start + LANES)
            total = g[p, 0, HALO : HALO + tile, span] + cols[j]
            total = jnp.concatenate(
                [
                    total[:HALO] + above[p, 0, :, span],
                    total[HALO:-HALO],
                    total[-HALO:] + below[p, 0, :, span],
                ],
                axis=0,
            )
            out[p, 0, :, span] = obj[p, 0, :, span] - STEP * total


def step_call(obj, g, lft, rgt, above, below, first, after):
    tile = obj.shape[2]
    count, rows = g.shape[1:3]
    side = lft.shape[2:]
    return pl.pallas_call(
        ordered(step_kernel, 6, after),
        grid=(count,),
        in_specs=[
            later(first, tile, tile),
            plane(rows, tile),
            plane(*side),
            plane(*side),
            plane(HALO, tile),
            plane(HALO, tile),
        ]
        + anywhere(after),
        out_specs=plane(tile, tile),
        out_shape=struct(2, count, tile, tile),
        compiler_params=params(),
        cost_estimate=cost(1e3, 1e3),
    )(obj, g, lft, rgt, above, below, *after)


def couple_kernel(table, choose, *refs):
    parts, out, weights = refs[:-2], refs[-2], refs[-1]
    energies = out.shape[1]
    spans = chunks_of(energies)
    width = choose.shape[1]

    @pl.when(pl.program_id(0) == 0)
    def _():
        rows = lax.broadcasted_iota(jnp.int32, (weights.shape[0], table.shape[0]), 0)
        source = lax.broadcasted_iota(jnp.int32, rows.shape, 1)
        spread = (rows // SUB == source).astype(jnp.bfloat16)
        wide = (weights.shape[0], width)
        lane = lax.broadcasted_iota(jnp.int32, wide, 1)
        same = lax.broadcasted_iota(jnp.int32, wide, 0) % SUB == lane % SUB
        for part, spots in zip(split(table[...]), ((0, 1), (2,))):
            picked = dot(part, choose[...]).astype(jnp.bfloat16)
            grown = jnp.where(same, dot(spread, picked), 0.0).astype(jnp.bfloat16)
            for spot in spots:
                weights[:, spot * width : (spot + 1) * width] = grown

    for g in range(out.shape[2] // SUB):
        rows = slice(g * SUB, (g + 1) * SUB)

        def flat(ref, q):
            x = ref[q, :, rows, :]
            return x.reshape(x.shape[0] * SUB, x.shape[2])

        own = [[flat(ref, q) for q in range(2)] for ref in parts[: len(spans)]]
        other = [[flat(ref, q) for q in range(2)] for ref in parts[len(spans) :]]
        hi, lo = split(jnp.concatenate([x for pair in own + other for x in pair], axis=0))
        mixed = dot(weights[...], jnp.concatenate([hi, lo, hi], axis=0))
        for (first, count), pair in zip(spans, own):
            for p in range(2):
                start = (p * energies + first) * SUB
                value = pair[p] + mixed[start : start + count * SUB]
                out[p, first : first + count, rows, :] = value.reshape(count, SUB, value.shape[1])


def couple_call(table, choose, parts, energies, after):
    tile = parts[0].shape[2]
    rows = 2 * SUB

    def block(count):
        return pl.BlockSpec((2, count, rows, tile), lambda i: (0, 0, i, 0))

    return pl.pallas_call(
        ordered(couple_kernel, 2 + len(parts), after),
        grid=(tile // rows,),
        in_specs=[
            pl.BlockSpec(table.shape, lambda i: (0, 0)),
            pl.BlockSpec(choose.shape, lambda i: (0, 0)),
        ]
        + [block(part.shape[1]) for part in parts]
        + anywhere(after),
        out_specs=block(energies),
        out_shape=struct(2, energies, tile, tile),
        scratch_shapes=[pltpu.VMEM((2 * energies * SUB, 3 * choose.shape[1]), jnp.bfloat16)],
        compiler_params=params(),
        cost_estimate=cost(1e3, 1e3),
    )(table, choose, *parts, *after)


def coupling(kk_kernel, energies):
    count = lax.axis_size("energy")
    me = lax.axis_index("energy")
    total = kk_kernel.shape[3]
    mine = lax.dynamic_slice_in_dim(kk_kernel, me * energies, energies, axis=2)
    table = mine.transpose(0, 2, 1, 3).reshape(2 * energies, 2 * total)
    shift, within, base = [], [], []
    for step in range(count):
        for first, size in chunks_of(energies):
            for q in range(2):
                for f in range(first, first + size):
                    shift += [step] * SUB
                    within += [f] * SUB
                    base += [q * total] * SUB
    source = (me - jnp.asarray(shift, jnp.int32)) % count
    column = jnp.asarray(base, jnp.int32) + source * energies + jnp.asarray(within, jnp.int32)
    row = lax.broadcasted_iota(jnp.int32, (2 * total, len(shift)), 0)
    return table, (row == column[None]).astype(jnp.bfloat16)


def toward(block, axis, distance):
    count = lax.axis_size(axis)
    route = [(i, i + distance) for i in range(count) if 0 <= i + distance < count]
    return lax.ppermute(block, axis, route)


def local(object_field, probe_field, amplitudes, kk_kernel, offsets):
    energies = object_field.shape[1]
    ring = lax.axis_size("energy")
    tables = [jnp.asarray(m) for m in dft_parts(probe_field.shape[2])]
    offs = offsets.reshape(-1)
    table, choose = coupling(kk_kernel, energies)
    tiles = lax.axis_size("row") * lax.axis_size("col")
    scales = (tiles, PROBE_STEP / (offsets.shape[2] * tiles))
    spans = chunks_of(energies)
    energy_route = lambda shift: [(i, (i + shift) % ring) for i in range(ring)]
    halos, grads, own = [], [], []
    other = [[] for _ in range(ring - 1)]
    for first, count in spans:
        part = object_field[:, first : first + count]
        top, bot = toward(part[:, :, -HALO:], "row", 1), toward(part[:, :, :HALO], "row", -1)
        left, right = pack_call(object_field, top, bot, first, count, [])
        halos.append((top, bot, toward(right, "col", 1), toward(left, "col", -1)))
    rims = []

    def trim(i):
        g, g_left, g_right = grads[i]
        lft = toward(g_right, "col", 1)
        rgt = toward(g_left, "col", -1)
        top, bot = rim_call(g, lft, rgt, [])
        rims.append((g, lft, rgt, toward(bot, "row", 1), toward(top, "row", -1)))
        return top

    running, after = [], []
    for i, ((first, count), halo) in enumerate(zip(spans, halos)):
        *grad, share = gradient_call(
            scales, offs, object_field, *halo, probe_field, amplitudes, *tables,
            first, count, running, after,
        )
        grads.append(grad)
        running, after = [share], []
        if i == len(spans) - 2:
            after = [trim(len(rims))]
    new_probe = lax.psum(share, ("row", "col"))
    for i, (first, count) in enumerate(spans):
        if i >= len(rims):
            trim(i)
        after = own[-1:]
        if i == len(spans) - 1:
            after = after + [group[0] for group in other]
        own.append(step_call(object_field, *rims[i], first, after))
        for shift in range(1, ring):
            other[shift - 1].append(lax.ppermute(own[-1], "energy", energy_route(shift)))
    other = [x for group in other for x in group]
    blended = couple_call(table, choose, own + other, energies, [])
    return (blended, new_probe)


def solution(mesh):
    return jax.shard_map(
        local,
        mesh=mesh,
        in_specs=(
            P(None, "energy", "row", "col"),
            P(None, "energy", None, None),
            P("energy", "row", "col", None, None, None),
            P(),
            P("row", "col", None, None),
        ),
        out_specs=(P(None, "energy", "row", "col"), P(None, "energy", None, None)),
        check_vma=False,
    )
```

```python
import math

import jax
import jax.numpy as jnp
import ml_dtypes
import numpy as np
from jax import lax
from jax.experimental import pallas as pl
from jax.experimental.pallas import tpu as pltpu
from jax.sharding import PartitionSpec as P

HALO = 64
LANES = 128
SUB = 8
STEP = 0.25
PROBE_STEP = 0.5
FLOOR = 0.25
PARTS = (5, 6, 5)
VMEM = 56 * 2**20


def chunks_of(energies):
    if energies == sum(PARTS):
        sizes = PARTS
    else:
        sizes = (1,) * energies
    return [(sum(sizes[:i]), size) for i, size in enumerate(sizes)]


def split(x):
    hi = x.astype(jnp.bfloat16)
    return hi, (x - hi.astype(jnp.float32)).astype(jnp.bfloat16)


def dft_parts(length):
    half = length // 2
    pixel = np.arange(half)
    even = pixel - pixel % 2 + half * (pixel % 2)
    out = []
    for freqs in (even, even + 1):
        angle = (freqs[:, None] * pixel[None, :] % length) * (2.0 * math.pi / length)
        c, s = np.cos(angle) / math.sqrt(length), np.sin(angle) / math.sqrt(length)
        m = np.block([[c, s], [-s, c]])
        hi = m.astype(np.float32).astype(ml_dtypes.bfloat16)
        lo = (m - hi.astype(np.float64)).astype(np.float32).astype(ml_dtypes.bfloat16)
        out.append((hi, lo))
    even, odd = out
    wide = lambda m: np.concatenate([m[0], m[0], m[1]], axis=1)
    tall = lambda m: np.concatenate([m[0], m[0], m[1]], axis=0)
    t = lambda m: (m[0].T, m[1].T)
    left = np.stack([wide(even), wide(odd), wide(t(even)), wide(t(odd))])
    right = np.stack([tall(t(even)), tall(t(odd)), tall(even), tall(odd)])
    return left, right


def dot(a, b):
    return jnp.dot(a, b, preferred_element_type=jnp.float32)


def gradient_kernel(
    tiles, rate, offs, obj, top, bot, lft, rgt, probe, amp, left, right, gout, gl, gr, pg, ext, grad
):
    win = probe.shape[2]
    tile = obj.shape[2]
    half = win // 2
    rows = tile + 2 * HALO
    mid = rows // 2
    lane = lax.broadcasted_iota(jnp.int32, (win, LANES), 1)
    for p in range(2):
        for j in range(tile // LANES):
            cols = slice(j * LANES, (j + 1) * LANES)
            ext[p, 1 + j, 0:HALO] = top[p, 0, :, cols]
            ext[p, 1 + j, HALO : HALO + tile] = obj[p, 0, :, cols]
            ext[p, 1 + j, HALO + tile : rows] = bot[p, 0, :, cols]
        packed = lft[p, 0]
        ext[p, 0, 0:mid] = pltpu.roll(packed, HALO, 1)
        ext[p, 0, mid:rows] = packed
        packed = rgt[p, 0]
        ext[p, 3, 0:mid] = packed
        ext[p, 3, mid:rows] = pltpu.roll(packed, HALO, 1)
    grad[...] = jnp.zeros_like(grad)
    pg[...] = jnp.zeros_like(pg)

    def window_of(k):
        a = offs[2 * k]
        b = offs[2 * k + 1] + HALO
        base = b // LANES
        r = b % LANES
        back = (LANES - r) % LANES
        return a, base, r, back

    def position(k):
        a, base, r, back = window_of(k)
        keep = lane < LANES - r
        def load(p):
            v = [pltpu.roll(ext[p, base + j, pl.ds(a, win), :], back, 1) for j in range(3)]
            return jnp.concatenate([jnp.where(keep, v[0], v[1]), jnp.where(keep, v[1], v[2])], axis=1)
        wr, wi = load(0), load(1)
        pr, pi = probe[0, 0], probe[1, 0]
        er = pr * wr - pi * wi
        ei = pr * wi + pi * wr

        def lmul(which, top_, bottom_):
            hi, lo = split(jnp.concatenate([top_, bottom_], axis=0))
            return dot(left[which], jnp.concatenate([hi, lo, hi], axis=0))

        def rmul(which, l_, r_):
            hi, lo = split(jnp.concatenate([l_, r_], axis=1))
            return dot(jnp.concatenate([hi, lo, hi], axis=1), right[which])

        ze = lmul(0, er[:half] + er[half:], ei[:half] + ei[half:])
        zo = lmul(1, er[:half] - er[half:], ei[:half] - ei[half:])
        zr = jnp.concatenate([ze[:half], zo[:half]], axis=0)
        zi = jnp.concatenate([ze[half:], zo[half:]], axis=0)
        ye = rmul(0, zr[:, :half] + zr[:, half:], zi[:, :half] + zi[:, half:])
        yo = rmul(1, zr[:, :half] - zr[:, half:], zi[:, :half] - zi[:, half:])
        meas = amp[0, 0, 0, k]
        groups = (half // 8, 8, win)
        mt, mb = meas[:half].reshape(groups), meas[half:].reshape(groups)
        odd_row = lax.broadcasted_iota(jnp.int32, groups, 1) % 2 == 1
        meas = jnp.concatenate(
            [
                jnp.where(odd_row, pltpu.roll(mb, 1, 1), mt).reshape(half, win),
                jnp.where(odd_row, mb, pltpu.roll(mt, 7, 1)).reshape(half, win),
            ],
            axis=0,
        )
        odd = lane % 2 == 1
        ml, mr = meas[:, :half], meas[:, half:]
        me = jnp.where(odd, pltpu.roll(mr, 1, 1), ml)
        mo = jnp.where(odd, mr, pltpu.roll(ml, LANES - 1, 1))

        def fix(y, m_):
            fr, fi = y[:, :half], y[:, half:]
            s = m_ * lax.rsqrt(jnp.maximum(fr * fr + fi * fi, FLOOR * FLOOR))
            return fr * s, fi * s

        te = rmul(2, *fix(ye, me))
        to = rmul(3, *fix(yo, mo))
        sr, dr = te[:, :half] + to[:, :half], te[:, :half] - to[:, :half]
        si, di = te[:, half:] + to[:, half:], te[:, half:] - to[:, half:]
        xr = jnp.concatenate([sr, dr], axis=1)
        xi = jnp.concatenate([si, di], axis=1)
        be = lmul(2, xr[:half], xi[:half])
        bo = lmul(3, xr[half:], xi[half:])
        br = jnp.concatenate([be[:half] + bo[:half], be[:half] - bo[:half]], axis=0)
        bi = jnp.concatenate([be[half:] + bo[half:], be[half:] - bo[half:]], axis=0)
        dr, di = er - br, ei - bi
        pg[0, 0] += wr * dr + wi * di
        pg[1, 0] += wr * di - wi * dr
        steps = (pr * dr + pi * di, pr * di - pi * dr)
        below = lane < r
        for p in range(2):
            u = pltpu.roll(steps[p][:, :LANES], r, 1)
            v = pltpu.roll(steps[p][:, LANES:], r, 1)
            grad[p, base, pl.ds(a, win), :] += jnp.where(below, 0.0, u)
            grad[p, base + 1, pl.ds(a, win), :] += jnp.where(below, u, v)
            grad[p, base + 2, pl.ds(a, win), :] += jnp.where(below, v, 0.0)

    for k in range(amp.shape[3]):
        position(k)
    pg[...] = probe[...] * (1.0 / tiles) - rate * pg[...]
    first = lax.broadcasted_iota(jnp.int32, (mid, LANES), 1) < HALO
    for p in range(2):
        for j in range(tile // LANES):
            gout[p, 0, :, j * LANES : (j + 1) * LANES] = grad[p, 1 + j]
        edge = grad.at[p, 0]
        gl[p, 0] = jnp.where(first, pltpu.roll(edge[0:mid], HALO, 1), edge[mid:rows])
        edge = grad.at[p, 3]
        gr[p, 0] = jnp.where(first, edge[0:mid], pltpu.roll(edge[mid:rows], HALO, 1))


def params():
    return pltpu.CompilerParams(vmem_limit_bytes=VMEM)


def cost(flops, moved):
    return pl.CostEstimate(flops=1000, bytes_accessed=1000, transcendentals=0)


def anywhere(arrays):
    return [pl.BlockSpec(memory_space=pl.ANY)] * len(arrays)


def ordered(kernel, inputs, after):
    def body(*refs):
        return kernel(*refs[:inputs], *refs[inputs + len(after) :])

    return body


def plane(*shape):
    return pl.BlockSpec((2, 1) + shape, lambda e, *_: (0, e, 0, 0))


def later(first, *shape):
    return pl.BlockSpec((2, 1) + shape, lambda e, *_: (0, first + e, 0, 0))


def struct(*shape):
    return jax.ShapeDtypeStruct(shape, jnp.float32)


def gradient_call(
    scales, offs, obj, top, bot, lft, rgt, probe, amp, left, right, first, count, running, after
):
    win, tile = probe.shape[2], obj.shape[2]
    rows = tile + 2 * HALO
    side = (rows // 2, LANES)
    frame = pltpu.VMEM((2, tile // LANES + 2, rows, LANES), jnp.float32)
    whole = lambda m: pl.BlockSpec(m.shape, lambda e, *_: (0, 0, 0))
    return pl.pallas_call(
        ordered(lambda *refs: gradient_kernel(*scales, *refs), 10, running + after),
        grid_spec=pltpu.PrefetchScalarGridSpec(
            num_scalar_prefetch=1,
            grid=(count,),
            in_specs=[
                later(first, tile, tile),
                plane(HALO, tile),
                plane(HALO, tile),
                plane(*side),
                plane(*side),
                later(first, win, win),
                pl.BlockSpec((1, 1, 1) + amp.shape[3:], lambda e, *_: (first + e, 0, 0, 0, 0, 0)),
                whole(left),
                whole(right),
            ]
            + anywhere(running + after),
            out_specs=[plane(rows, tile), plane(*side), plane(*side), later(first, win, win)],
            scratch_shapes=[frame, frame],
        ),
        out_shape=[
            struct(2, count, rows, tile),
            struct(2, count, *side),
            struct(2, count, *side),
            struct(*probe.shape),
        ],
        input_output_aliases={10: 3} if running else {},
        compiler_params=params(),
        cost_estimate=cost(count * 7e9, count * 5e6),
    )(offs, obj, top, bot, lft, rgt, probe, amp, left, right, *running, *after)


def pack_kernel(near, far, top_near, top_far, bot_near, bot_far, left, right):
    tile = near.shape[2]
    mid = tile // 2
    for p in range(2):
        for refs, out, low in (
            ((top_near, near, bot_near), left, True),
            ((top_far, far, bot_far), right, False),
        ):
            body = refs[1][p, 0]
            upper = jnp.concatenate([refs[0][p, 0], body[:mid]], axis=0)
            lower = jnp.concatenate([body[mid:], refs[2][p, 0]], axis=0)
            lane = lax.broadcasted_iota(jnp.int32, upper.shape, 1)
            if low:
                out[p, 0] = jnp.where(lane < HALO, upper, pltpu.roll(lower, HALO, 1))
            else:
                out[p, 0] = jnp.where(lane < HALO, pltpu.roll(upper, HALO, 1), lower)


def pack_call(obj, top, bot, first, count, after):
    tile = obj.shape[2]
    last = tile // LANES - 1
    side = (tile // 2 + HALO, LANES)

    def lanes(rows, base, block):
        return pl.BlockSpec((2, 1, rows, LANES), lambda e: (0, base + e, 0, block))

    return pl.pallas_call(
        ordered(pack_kernel, 6, after),
        grid=(count,),
        in_specs=[
            lanes(tile, first, 0),
            lanes(tile, first, last),
            lanes(HALO, 0, 0),
            lanes(HALO, 0, last),
            lanes(HALO, 0, 0),
            lanes(HALO, 0, last),
        ]
        + anywhere(after),
        out_specs=[plane(*side), plane(*side)],
        out_shape=[struct(2, count, *side)] * 2,
        compiler_params=params(),
        cost_estimate=cost(0, count * 12e5),
    )(obj, obj, top, top, bot, bot, *after)


def from_left(packed, upper):
    lane = lax.broadcasted_iota(jnp.int32, packed.shape, 1)
    return jnp.where(lane < HALO, packed if upper else pltpu.roll(packed, HALO, 1), 0.0)


def from_right(packed, upper):
    lane = lax.broadcasted_iota(jnp.int32, packed.shape, 1)
    return jnp.where(lane < HALO, 0.0, pltpu.roll(packed, HALO, 1) if upper else packed)


def rim_kernel(g_top, g_bot, l_top, l_bot, r_top, r_bot, top, bot):
    for p in range(2):
        for g, l, r, out, upper in (
            (g_top, l_top, r_top, top, True),
            (g_bot, l_bot, r_bot, bot, False),
        ):
            out[p, 0] = g[p, 0]
            out[p, 0, :, :LANES] += from_left(l[p, 0], upper)
            out[p, 0, :, -LANES:] += from_right(r[p, 0], upper)


def rim_call(g, lft, rgt, after):
    count, rows, tile = g.shape[1:]

    def strip(block, width):
        return pl.BlockSpec((2, 1, HALO, width), lambda e: (0, e, block, 0))

    last = rows // HALO - 1
    packed_last = lft.shape[2] // HALO - 1
    return pl.pallas_call(
        ordered(rim_kernel, 6, after),
        grid=(count,),
        in_specs=[
            strip(0, tile),
            strip(last, tile),
            strip(0, LANES),
            strip(packed_last, LANES),
            strip(0, LANES),
            strip(packed_last, LANES),
        ]
        + anywhere(after),
        out_specs=[plane(HALO, tile), plane(HALO, tile)],
        out_shape=[struct(2, count, HALO, tile)] * 2,
        compiler_params=params(),
        cost_estimate=cost(1e3, 1e3),
    )(g, g, lft, lft, rgt, rgt, *after)


def step_kernel(obj, g, lft, rgt, above, below, out):
    tile = obj.shape[2]
    mid = tile // 2
    for p in range(2):
        l, r = lft[p, 0], rgt[p, 0]
        cols = (
            jnp.concatenate([from_left(l, True)[HALO:], from_left(l, False)[:mid]], axis=0),
            jnp.concatenate([from_right(r, True)[HALO:], from_right(r, False)[:mid]], axis=0),
        )
        for j, start in enumerate((0, tile - LANES)):
            span = slice(start, start + LANES)
            total = g[p, 0, HALO : HALO + tile, span] + cols[j]
            total = jnp.concatenate(
                [
                    total[:HALO] + above[p, 0, :, span],
                    total[HALO:-HALO],
                    total[-HALO:] + below[p, 0, :, span],
                ],
                axis=0,
            )
            out[p, 0, :, span] = obj[p, 0, :, span] - STEP * total


def step_call(obj, g, lft, rgt, above, below, first, after):
    tile = obj.shape[2]
    count, rows = g.shape[1:3]
    side = lft.shape[2:]
    return pl.pallas_call(
        ordered(step_kernel, 6, after),
        grid=(count,),
        in_specs=[
            later(first, tile, tile),
            plane(rows, tile),
            plane(*side),
            plane(*side),
            plane(HALO, tile),
            plane(HALO, tile),
        ]
        + anywhere(after),
        out_specs=plane(tile, tile),
        out_shape=struct(2, count, tile, tile),
        compiler_params=params(),
        cost_estimate=cost(1e3, 1e3),
    )(obj, g, lft, rgt, above, below, *after)


def couple_kernel(table, choose, *refs):
    parts, out, weights = refs[:-2], refs[-2], refs[-1]
    energies = out.shape[1]
    spans = chunks_of(energies)
    width = choose.shape[1]

    @pl.when(pl.program_id(0) == 0)
    def _():
        rows = lax.broadcasted_iota(jnp.int32, (weights.shape[0], table.shape[0]), 0)
        source = lax.broadcasted_iota(jnp.int32, rows.shape, 1)
        spread = (rows // SUB == source).astype(jnp.bfloat16)
        wide = (weights.shape[0], width)
        lane = lax.broadcasted_iota(jnp.int32, wide, 1)
        same = lax.broadcasted_iota(jnp.int32, wide, 0) % SUB == lane % SUB
        for part, spots in zip(split(table[...]), ((0, 1), (2,))):
            picked = dot(part, choose[...]).astype(jnp.bfloat16)
            grown = jnp.where(same, dot(spread, picked), 0.0).astype(jnp.bfloat16)
            for spot in spots:
                weights[:, spot * width : (spot + 1) * width] = grown

    for g in range(out.shape[2] // SUB):
        rows = slice(g * SUB, (g + 1) * SUB)

        def flat(ref, q):
            x = ref[q, :, rows, :]
            return x.reshape(x.shape[0] * SUB, x.shape[2])

        own = [[flat(ref, q) for q in range(2)] for ref in parts[: len(spans)]]
        other = [[flat(ref, q) for q in range(2)] for ref in parts[len(spans) :]]
        hi, lo = split(jnp.concatenate([x for pair in own + other for x in pair], axis=0))
        mixed = dot(weights[...], jnp.concatenate([hi, lo, hi], axis=0))
        for (first, count), pair in zip(spans, own):
            for p in range(2):
                start = (p * energies + first) * SUB
                value = pair[p] + mixed[start : start + count * SUB]
                out[p, first : first + count, rows, :] = value.reshape(count, SUB, value.shape[1])


def couple_call(table, choose, parts, energies, after):
    tile = parts[0].shape[2]
    rows = 2 * SUB

    def block(count):
        return pl.BlockSpec((2, count, rows, tile), lambda i: (0, 0, i, 0))

    return pl.pallas_call(
        ordered(couple_kernel, 2 + len(parts), after),
        grid=(tile // rows,),
        in_specs=[
            pl.BlockSpec(table.shape, lambda i: (0, 0)),
            pl.BlockSpec(choose.shape, lambda i: (0, 0)),
        ]
        + [block(part.shape[1]) for part in parts]
        + anywhere(after),
        out_specs=block(energies),
        out_shape=struct(2, energies, tile, tile),
        scratch_shapes=[pltpu.VMEM((2 * energies * SUB, 3 * choose.shape[1]), jnp.bfloat16)],
        compiler_params=params(),
        cost_estimate=cost(1e3, 1e3),
    )(table, choose, *parts, *after)


def coupling(kk_kernel, energies):
    count = lax.axis_size("energy")
    me = lax.axis_index("energy")
    total = kk_kernel.shape[3]
    mine = lax.dynamic_slice_in_dim(kk_kernel, me * energies, energies, axis=2)
    table = mine.transpose(0, 2, 1, 3).reshape(2 * energies, 2 * total)
    shift, within, base = [], [], []
    for step in range(count):
        for first, size in chunks_of(energies):
            for q in range(2):
                for f in range(first, first + size):
                    shift += [step] * SUB
                    within += [f] * SUB
                    base += [q * total] * SUB
    source = (me - jnp.asarray(shift, jnp.int32)) % count
    column = jnp.asarray(base, jnp.int32) + source * energies + jnp.asarray(within, jnp.int32)
    row = lax.broadcasted_iota(jnp.int32, (2 * total, len(shift)), 0)
    return table, (row == column[None]).astype(jnp.bfloat16)


def toward(block, axis, distance):
    count = lax.axis_size(axis)
    route = [(i, i + distance) for i in range(count) if 0 <= i + distance < count]
    return lax.ppermute(block, axis, route)


def local(object_field, probe_field, amplitudes, kk_kernel, offsets):
    energies = object_field.shape[1]
    ring = lax.axis_size("energy")
    tables = [jnp.asarray(m) for m in dft_parts(probe_field.shape[2])]
    offs = offsets.reshape(-1)
    table, choose = coupling(kk_kernel, energies)
    tiles = lax.axis_size("row") * lax.axis_size("col")
    scales = (tiles, PROBE_STEP / (offsets.shape[2] * tiles))
    spans = chunks_of(energies)
    energy_route = lambda shift: [(i, (i + shift) % ring) for i in range(ring)]
    halos, grads, own = [], [], []
    other = [[] for _ in range(ring - 1)]
    for first, count in spans:
        part = object_field[:, first : first + count]
        top, bot = toward(part[:, :, -HALO:], "row", 1), toward(part[:, :, :HALO], "row", -1)
        left, right = pack_call(object_field, top, bot, first, count, [])
        halos.append((top, bot, toward(right, "col", 1), toward(left, "col", -1)))
    rims = []

    def trim(i):
        g, g_left, g_right = grads[i]
        lft = toward(g_right, "col", 1)
        rgt = toward(g_left, "col", -1)
        top, bot = rim_call(g, lft, rgt, [])
        rims.append((g, lft, rgt, toward(bot, "row", 1), toward(top, "row", -1)))
        return top

    running, after = [], []
    for i, ((first, count), halo) in enumerate(zip(spans, halos)):
        *grad, share = gradient_call(
            scales, offs, object_field, *halo, probe_field, amplitudes, *tables,
            first, count, running, after,
        )
        grads.append(grad)
        running, after = [share], []
        if i == len(spans) - 2:
            after = [trim(len(rims))]
    new_probe = lax.psum(share, ("row", "col"))
    for i, (first, count) in enumerate(spans):
        if i >= len(rims):
            trim(i)
        after = own[-1:] or [x[1] for x in grads[1:2]]
        if i == len(spans) - 1:
            after = after + [group[0] for group in other]
        own.append(step_call(object_field, *rims[i], first, after))
        for shift in range(1, ring):
            other[shift - 1].append(lax.ppermute(own[-1], "energy", energy_route(shift)))
    other = [x for group in other for x in group]
    blended = couple_call(table, choose, own + other, energies, [])
    return (blended, new_probe)


def solution(mesh):
    return jax.shard_map(
        local,
        mesh=mesh,
        in_specs=(
            P(None, "energy", "row", "col"),
            P(None, "energy", None, None),
            P("energy", "row", "col", None, None, None),
            P(),
            P("row", "col", None, None),
        ),
        out_specs=(P(None, "energy", "row", "col"), P(None, "energy", None, None)),
        check_vma=False,
    )
```
